128 devices in a mesh: leaf: 64 (over z, y, x), rep: 2 (over core).
Axes of the slice: x: 4, y: 4, z: 4, core: 2. Of those that a mesh axis runs over, the one named last changes fastest.
Arguments:
- queries: bfloat16 [16384, 3584], P(('rep', 'leaf')), parts along dimension 0, may hold values from -64 to 64
- branch_key_value: bfloat16 [2, 16384, 512], P(None, ('rep', 'leaf')), parts along dimension 1, may hold values from -5 to 5
- prompt_key_value: bfloat16 [2, 16384, 512], P(None, ('rep', 'leaf')), parts along dimension 1, may hold values from -5 to 5
- parents: int32 [128], P('rep'), parts along dimension 0, may hold values from -1 to 62, as said below
- counts: int32 [128], P('rep'), parts along dimension 0, may hold values from 1 to 128, as said below
Outputs:
- attended: bfloat16 [16384, 3584], P(('rep', 'leaf')), parts along dimension 0
The draws below stay inside these ranges and needn't reach their ends.
There are 2 independent parts, one for each index of `rep`. The reference program is written for one: setup_inputs(seed, part) draws one part's arguments, and reference() takes and returns one part's arrays. A program takes and returns all parts, laid end to end along the dimension named above; each array names one. Nothing has to cross between parts.
Inputs may be any that keep to these rules, and one draw needn't show every extreme that they name: parents[b] is below b; parents[b] is -1 or at least 4 * (b // 4), so every tree lies within one aligned run of 4 blocks; the last block of every such run has the run's first block as parent; parents[0] is -1. counts[0] is 128.
All inputs are finite; a program needn't handle non-finite values.
Results may differ from the reference program's by a relative error of at most 0.0095.
Values may be sent and summed in bfloat16 or wider, within the bound.
A program may use at most 320 MiB of HBM per device.

```python
import jax
import jax.numpy as jnp
from jax import lax

QUERY_HEADS = 28
KEY_VALUE_HEADS = 4
HEAD_SIZE = 128
BLOCK_TOKENS = 128
REACH = 4
BLK_DEV = 1
TREE_BLOCKS = 64
PROMPT_BLOCKS = 64


def shared_root_keys(key):
    unscaled_scores = jax.random.normal(key, (PROMPT_BLOCKS * BLOCK_TOKENS, KEY_VALUE_HEADS * HEAD_SIZE), jnp.float32)
    return jnp.clip(unscaled_scores, -5.0, 5.0)


def draw_prompt_key_value(key, part):
    prompt_keys = shared_root_keys(key)
    key = jax.random.fold_in(key, 1)
    value_rows = jnp.clip(jax.random.normal(key, (PROMPT_BLOCKS * BLOCK_TOKENS, KEY_VALUE_HEADS * HEAD_SIZE), jnp.float32), -5.0, 5.0)
    return jnp.stack([prompt_keys, value_rows]).astype(jnp.bfloat16)


def draw_queries(key, part):
    key = jax.random.fold_in(key, 2)
    base = jax.random.normal(key, (TREE_BLOCKS * BLOCK_TOKENS, QUERY_HEADS * HEAD_SIZE), jnp.float32)
    return jnp.clip(base, -64.0, 64.0).astype(jnp.bfloat16)


def draw_parents(key, part):
    key = jax.random.fold_in(key, 3)
    index = jnp.arange(TREE_BLOCKS, dtype=jnp.int32)
    span_blocks = REACH * BLK_DEV
    first = index // span_blocks * span_blocks
    drawn = jax.random.randint(key, (TREE_BLOCKS,), first - 1, jnp.maximum(index, first), dtype=jnp.int32)
    drawn = jnp.where(drawn < first, -1, drawn)
    drawn = jnp.where(index % span_blocks == span_blocks - 1, first, drawn)
    return drawn


def draw_counts(key, part):
    key = jax.random.fold_in(key, 4)
    drawn = jax.random.randint(key, (TREE_BLOCKS,), 1, BLOCK_TOKENS + 1, dtype=jnp.int32)
    return drawn.at[0].set(BLOCK_TOKENS)


def block_levels(stream_key, shape, cuts, smallest, high):
    def one(dim, shards_of):
        draws = jax.random.uniform(jax.random.fold_in(jax.random.fold_in(stream_key, 6), dim), (shards_of,), jnp.float32, smallest / len(cuts), high / len(cuts))
        return jnp.repeat(jnp.exp(draws), shape[dim] // shards_of).reshape((-1,) + (1,) * (len(shape) - dim - 1))

    factor_of = one(*cuts[0])
    for cut in cuts[1:]:
        factor_of = factor_of * one(*cut)
    return factor_of


def scatter_about(key, extent, width, limit, pieces=(), held_as=jnp.bfloat16):
    values = width * jax.random.normal(key, extent, jnp.float32)
    if pieces:
        values = values * block_levels(key, extent, pieces, -0.22, 0.18)
    return jnp.clip(values, -limit, limit).astype(held_as)


def setup_inputs(seed: int = 0, part: int = 0) -> dict:
    arg_keys = jax.random.split(jax.random.key(seed), 6)
    own_keys = jax.random.split(jax.random.fold_in(arg_keys[5], part), 6)
    queries = draw_queries(jax.random.fold_in(jax.random.fold_in(arg_keys[5], part), 71), part)
    branch_key_value = scatter_about(own_keys[1], (2, TREE_BLOCKS * BLOCK_TOKENS, KEY_VALUE_HEADS * HEAD_SIZE), 1.0, 5.0, ((1, 64),))
    prompt_key_value = draw_prompt_key_value(jax.random.fold_in(jax.random.fold_in(arg_keys[5], part), 71), part)
    parents = draw_parents(jax.random.fold_in(jax.random.fold_in(arg_keys[5], part), 71), part)
    counts = draw_counts(jax.random.fold_in(jax.random.fold_in(arg_keys[5], part), 71), part)
    return {"queries": queries, "branch_key_value": branch_key_value, "prompt_key_value": prompt_key_value, "parents": parents, "counts": counts}


def ancestry_table(parents, total_blocks):
    index = jnp.arange(total_blocks, dtype=jnp.int32)
    onehot = (parents[:, None] == index[None, :]).astype(jnp.float32)

    def advance(step, state):
        reach, gathered = state
        reach = jnp.dot(reach, onehot, precision=lax.Precision.HIGHEST)
        return reach, gathered + reach

    reach, gathered = lax.fori_loop(0, total_blocks, advance, (onehot, onehot))
    return (gathered > 0.5).astype(jnp.float32)


def reference(queries, branch_key_value, prompt_key_value, parents, counts):
    total_blocks = parents.shape[0]
    group_index = QUERY_HEADS // KEY_VALUE_HEADS
    scale = HEAD_SIZE ** -0.5
    table = ancestry_table(parents, total_blocks)
    prompt_length = prompt_key_value.shape[1]
    branch_length = branch_key_value.shape[1]
    every_key_row = jnp.concatenate([prompt_key_value[0], branch_key_value[0]], axis=0).reshape(prompt_length + branch_length, KEY_VALUE_HEADS, HEAD_SIZE).astype(jnp.float32)
    every_value_row = jnp.concatenate([prompt_key_value[1], branch_key_value[1]], axis=0).reshape(prompt_length + branch_length, KEY_VALUE_HEADS, HEAD_SIZE).astype(jnp.float32)
    slot = jnp.arange(branch_length, dtype=jnp.int32)
    key_block = slot // BLOCK_TOKENS
    key_pos = slot % BLOCK_TOKENS
    key_live = key_pos < counts[key_block]
    positions = jnp.arange(BLOCK_TOKENS, dtype=jnp.int32)

    def one_block(block):
        query_rows = lax.dynamic_slice_in_dim(queries, (block * BLOCK_TOKENS).astype(jnp.int32), BLOCK_TOKENS, 0)
        query_rows = query_rows.reshape(BLOCK_TOKENS, KEY_VALUE_HEADS, group_index, HEAD_SIZE).astype(jnp.float32)
        seen_tree = (table[block][key_block] > 0.5) & key_live
        own = (key_block[None, :] == block) & (key_pos[None, :] <= positions[:, None])
        seen_tree = seen_tree[None, :] | own
        seen = jnp.concatenate([jnp.ones((BLOCK_TOKENS, prompt_length), dtype=bool), seen_tree], axis=1)
        scores = jnp.einsum("rkgd,nkd->rkgn", query_rows, every_key_row) * scale
        scores = jnp.where(seen[:, None, None, :], scores, -1e30)
        top = jnp.max(scores, axis=-1, keepdims=True)
        expo = jnp.where(seen[:, None, None, :], jnp.exp(scores - top), 0.0)
        total = jnp.sum(expo, axis=-1)
        weights = expo.astype(jnp.bfloat16).astype(jnp.float32)
        summed = jnp.einsum("rkgn,nkd->rkgd", weights, every_value_row)
        result = summed / total[..., None]
        live = positions < counts[block]
        result = jnp.where(live[:, None, None, None], result, 0.0)
        return result.reshape(BLOCK_TOKENS, QUERY_HEADS * HEAD_SIZE).astype(jnp.bfloat16)

    blocks = lax.map(one_block, jnp.arange(total_blocks, dtype=jnp.int32))
    return blocks.reshape(total_blocks * BLOCK_TOKENS, QUERY_HEADS * HEAD_SIZE)
```

```python
import functools
import math

import jax
import jax.numpy as jnp
from jax import lax
from jax.experimental import pallas as pl
from jax.experimental.pallas import tpu as pltpu
from jax.sharding import PartitionSpec as P

QUERY_HEADS = 28
KV_HEADS = 4
HEAD = 128
BLOCK = 128
LINE = 4
GROUP = QUERY_HEADS // KV_HEADS
WIDTH = GROUP * HEAD
ROWS = GROUP * BLOCK
RING = 16
HALF = RING // 2
OWN = LINE * BLOCK
PART = OWN // 2
STEP = 4 * PART
PROMPT = RING * OWN
TO_EXP2 = HEAD**-0.5 * math.log2(math.e)
LOWEST = -1e30
MESH = pl.DeviceIdType.MESH

SEM_PROMPT, SEM_TREE, SEM_QUERY, SEM_OUT, SEM_RING = 0, 4, 8, 12, 16
SEMS = SEM_RING + 4 * HALF


def shift_of(slot):
    return slot + slot // 2 - 2 * (slot // 3)


def kernel(queries, branch, prompt, parents, counts, out, q_buf, kv, tree, top, total, acc, stage, send_sem, recv_sem, local_sem):
    leaf = lax.axis_index("leaf")
    x = lax.rem(leaf, LINE)
    line = leaf - x
    y = lax.rem(leaf // LINE, LINE)
    z = leaf // (LINE * LINE)

    def ring_places(outer, inner):
        place = LINE * outer + lax.rem(inner + outer, LINE)
        found = []
        for turn in (1, RING - 1):
            there = lax.rem(place + turn, RING)
            far = there // LINE
            found.append((far, lax.rem(lax.rem(there, LINE) + 3 * far, LINE)))
        return found

    ring_devices = [[(a * LINE + b) * LINE + x for a, b in ring_places(z, y)],
                    [(b * LINE + a) * LINE + x for a, b in ring_places(y, z)]]
    line_devices = [line + lax.rem(x + d, LINE) for d in range(1, LINE)]

    barrier = pltpu.get_barrier_semaphore()
    partners = line_devices + ring_devices[0] + ring_devices[1]
    for device in partners:
        pl.semaphore_signal(barrier, inc=1, device_id={"leaf": device}, device_id_type=MESH)

    def columns(place, width):
        return pl.ds(pl.multiple_of(place * width, width), width)

    own_prompt = pltpu.make_async_copy(prompt.at[:, :, columns(x, HEAD)], kv.at[:, pl.ds(0, BLOCK), :], local_sem.at[0])
    own_query = pltpu.make_async_copy(queries.at[:, columns(x, WIDTH)], q_buf.at[0], local_sem.at[1])
    own_tree = pltpu.make_async_copy(branch.at[:, :, columns(x, HEAD)], tree.at[:, pl.ds(0, BLOCK), :], local_sem.at[2])
    own_out = pltpu.make_async_copy(stage.at[0], out.at[:, columns(x, WIDTH)], local_sem.at[3])
    own_prompt.start()
    own_query.start()
    own_tree.start()
    pl.semaphore_wait(barrier, len(partners))

    def to_line(slot, source, target, first):
        there = lax.rem(x + shift_of(slot), LINE)
        return pltpu.make_async_remote_copy(
            src_ref=source(there), dst_ref=target, send_sem=send_sem.at[first + slot], recv_sem=recv_sem.at[first + slot],
            device_id={"leaf": line + there}, device_id_type=MESH)

    def prompt_copy(slot):
        return to_line(slot, lambda there: prompt.at[:, :, columns(there, HEAD)], kv.at[:, pl.ds(slot * BLOCK, BLOCK), :], SEM_PROMPT)

    def tree_copy(slot):
        return to_line(slot, lambda there: branch.at[:, :, columns(there, HEAD)], tree.at[:, pl.ds(slot * BLOCK, BLOCK), :], SEM_TREE)

    def query_copy(slot):
        return to_line(slot, lambda there: queries.at[:, columns(there, WIDTH)], q_buf.at[slot], SEM_QUERY)

    def out_copy(slot):
        there = lax.rem(x - shift_of(slot) + LINE, LINE)
        return pltpu.make_async_remote_copy(
            src_ref=stage.at[slot], dst_ref=out.at[:, columns(x, WIDTH)], send_sem=send_sem.at[SEM_OUT + slot],
            recv_sem=recv_sem.at[SEM_OUT + slot], device_id={"leaf": line + there}, device_id_type=MESH)

    def region(step, stream):
        if step == 0:
            return pl.ds(stream // 2 * PART, PART)
        if step < HALF:
            return pl.ds(OWN + (step - 1) * STEP + stream * PART, PART)
        return pl.ds(OWN + (HALF - 1) * STEP + stream * (PART // 2), PART // 2)

    def ring_copy(step, stream):
        source = region(step - 1, stream)
        if step == HALF:
            source = pl.ds(source.start + stream % 2 * (PART // 2), PART // 2)
        sem = SEM_RING + (step - 1) * 4 + stream
        return pltpu.make_async_remote_copy(
            src_ref=kv.at[:, source, :], dst_ref=kv.at[:, region(step, stream), :], send_sem=send_sem.at[sem],
            recv_sem=recv_sem.at[sem], device_id={"leaf": ring_devices[stream // 2][stream % 2]}, device_id_type=MESH)

    def advance(step):
        for stream in range(4):
            if step:
                ring_copy(step, stream).wait_recv()
            if step < HALF:
                ring_copy(step + 1, stream).start()

    for slot in (1, 2, 3):
        prompt_copy(slot).start()
    for slot in (1, 2):
        query_copy(slot).start()
    for slot in (1, 2, 3):
        tree_copy(slot).start()
    query_copy(3).start()

    parent = [parents[line + i] - line for i in range(LINE)]
    above = {}
    for b in range(1, LINE):
        for c in range(b):
            seen = jnp.where(parent[b] == c, 1, 0)
            for mid in range(c + 1, b):
                seen = jnp.maximum(seen, jnp.where(parent[b] == mid, above[mid, c], 0))
            above[b, c] = seen

    def masked(scores, slot):
        mine = lax.rem(x - shift_of(slot) + LINE, LINE)
        row = lax.broadcasted_iota(jnp.int32, (BLOCK, BLOCK), 0)
        column = lax.broadcasted_iota(jnp.int32, (BLOCK, BLOCK), 1)
        heads = [[] for _ in range(GROUP)]
        for other in range(LINE):
            block = lax.rem(x - shift_of(other) + LINE, LINE)
            linked = jnp.int32(0)
            for (b, c), seen in above.items():
                linked = jnp.where((mine == b) & (block == c), seen, linked)
            limit = linked * counts[line + block]
            limits = jnp.where(mine == block, row + 1, limit)
            for g in range(GROUP):
                piece = scores[g * BLOCK:(g + 1) * BLOCK, other * BLOCK:(other + 1) * BLOCK]
                heads[g].append(jnp.where(column < limits, piece, LOWEST))
        return jnp.concatenate([jnp.concatenate(head, axis=1) for head in heads], axis=0)

    def score(q, keys):
        return lax.dot_general(q, keys, (((1,), (1,)), ((), ())), preferred_element_type=jnp.float32)

    def attend(slot, chunks, first=False, last=False):
        q = jnp.concatenate([q_buf[slot, :, g * HEAD:(g + 1) * HEAD] for g in range(GROUP)], axis=0)
        if first:
            m, l, a = jnp.full((ROWS, HEAD), LOWEST, jnp.float32), jnp.zeros((ROWS, HEAD), jnp.float32), jnp.zeros((ROWS, HEAD), jnp.float32)
        else:
            m, l, a = top[slot], total[slot], acc[slot]

        def scores_of(chunk):
            buffer, start, length = chunk
            s = score(q, buffer[0, pl.ds(start, length), :])
            return masked(s, slot) if buffer is tree else s

        s = scores_of(chunks[0])
        for n, (buffer, start, length) in enumerate(chunks):
            following = scores_of(chunks[n + 1]) if n + 1 < len(chunks) else None
            new = jnp.maximum(m, jnp.broadcast_to(jnp.max(s, axis=1, keepdims=True), (ROWS, HEAD)))
            factor = jnp.exp2((m - new) * TO_EXP2)
            weights = jnp.concatenate(
                [jnp.exp2((s[:, i:i + HEAD] - new) * TO_EXP2).astype(jnp.bfloat16) for i in range(0, length, HEAD)], axis=1)
            values = buffer[1, pl.ds(start, length), :]
            both = jnp.dot(weights, jnp.concatenate([values, jnp.ones_like(values)], axis=1), preferred_element_type=jnp.float32)
            a = a * factor + both[:, :HEAD]
            l = l * factor + both[:, HEAD:]
            m, s = new, following
        if not last:
            top[slot], total[slot], acc[slot] = m, l, a
            return
        mine = lax.rem(x - shift_of(slot) + LINE, LINE)
        live = lax.broadcasted_iota(jnp.int32, (BLOCK, HEAD), 0) < counts[line + mine]
        for g in range(GROUP):
            rows = slice(g * BLOCK, (g + 1) * BLOCK)
            stage[slot, :, g * HEAD:(g + 1) * HEAD] = jnp.where(live, a[rows] / l[rows], 0.0).astype(stage.dtype)

    def ring_chunks(steps, length):
        start, end = OWN + (steps[0] - 1) * STEP, min(OWN + steps[-1] * STEP, PROMPT)
        return [(kv, at, min(length, end - at)) for at in range(start, end, length)]

    beginning = [(kv, 0, OWN), (tree, 0, OWN)]

    own_prompt.wait()
    for slot in (1, 2, 3):
        prompt_copy(slot).wait_recv()
    advance(0)
    own_query.wait()
    own_tree.wait()
    for slot in (1, 2, 3):
        tree_copy(slot).wait_recv()
    attend(0, beginning, first=True)
    advance(1)
    for slot in (1, 2):
        query_copy(slot).wait_recv()

    def two(i, c):
        attend(i + 1, beginning + ring_chunks((1,), 1024), first=True)
        return c

    lax.fori_loop(0, 2, two, 0)
    attend(0, ring_chunks((1,), 512))
    advance(2)

    def three(i, c):
        attend(i, ring_chunks((2,), 512))
        return c

    lax.fori_loop(0, 3, three, 0)
    advance(3)
    query_copy(3).wait_recv()
    attend(3, beginning + ring_chunks((1, 2), 1024), first=True)
    advance(4)

    def four(i, c):
        attend(i, ring_chunks((3, 4), 1024))

        @pl.when(i == 1)
        def _():
            advance(5)

        @pl.when(i == 2)
        def _():
            advance(6)

        return c

    lax.fori_loop(0, 4, four, 0)
    advance(7)
    advance(8)

    def final(i, c):
        slot = 3 - i
        attend(slot, ring_chunks((5, 6, 7, 8), 1024), last=True)

        @pl.when(i < 3)
        def _():
            out_copy(slot).start()

        return c

    lax.fori_loop(0, 4, final, 0)
    own_out.start()
    for slot in (1, 2, 3):
        prompt_copy(slot).wait_send()
        tree_copy(slot).wait_send()
        query_copy(slot).wait_send()
        out_copy(slot).wait_send()
    for step in range(1, HALF + 1):
        for stream in range(4):
            ring_copy(step, stream).wait_send()
    for slot in (1, 2, 3):
        out_copy(slot).wait_recv()
    own_out.wait()


def shards(queries, branch, prompt, parents, counts):
    return pl.pallas_call(
        kernel,
        out_shape=jax.ShapeDtypeStruct(queries.shape, queries.dtype),
        in_specs=[pl.BlockSpec(memory_space=pl.ANY)] * 3 + [pl.BlockSpec(memory_space=pltpu.SMEM)] * 2,
        out_specs=pl.BlockSpec(memory_space=pl.ANY),
        scratch_shapes=[
            pltpu.VMEM((LINE, BLOCK, WIDTH), jnp.bfloat16),
            pltpu.VMEM((2, PROMPT, HEAD), jnp.bfloat16),
            pltpu.VMEM((2, OWN, HEAD), jnp.bfloat16),
            pltpu.VMEM((LINE, ROWS, HEAD), jnp.float32),
            pltpu.VMEM((LINE, ROWS, HEAD), jnp.float32),
            pltpu.VMEM((LINE, ROWS, HEAD), jnp.float32),
            pltpu.VMEM((LINE, BLOCK, WIDTH), jnp.bfloat16),
            pltpu.SemaphoreType.DMA((SEMS,)),
            pltpu.SemaphoreType.DMA((SEMS,)),
            pltpu.SemaphoreType.DMA((4,)),
        ],
        compiler_params=pltpu.CompilerParams(
            collective_id=0, has_side_effects=True, vmem_limit_bytes=52 * 2**20
        ),
    )(queries, branch, prompt, parents, counts)


def solution(mesh):
    placed = (
        P(("rep", "leaf"), None),
        P(None, ("rep", "leaf"), None),
        P(None, ("rep", "leaf"), None),
        P("rep"),
        P("rep"),
    )
    return jax.shard_map(
        shards, mesh=mesh, in_specs=placed, out_specs=P(("rep", "leaf"), None), check_vma=False
    )
```

```python
import functools
import math

import jax
import jax.numpy as jnp
from jax import lax
from jax.experimental import pallas as pl
from jax.experimental.pallas import tpu as pltpu
from jax.sharding import PartitionSpec as P

QUERY_HEADS = 28
KV_HEADS = 4
HEAD = 128
BLOCK = 128
LINE = 4
GROUP = QUERY_HEADS // KV_HEADS
WIDTH = GROUP * HEAD
ROWS = GROUP * BLOCK
PLANE = 16
PEERS = 6
RELAYS = 18
PROMPT = PLANE * LINE * BLOCK
REST = (LINE - 1) * BLOCK
AT_PEERS = BLOCK
AT_REST = AT_PEERS + PEERS * BLOCK
AT_RELAYS = AT_REST + REST
AT_REST_PEERS = AT_RELAYS + RELAYS * BLOCK // 2
AT_REST_RELAYS = AT_REST_PEERS + PEERS * REST
TO_EXP2 = HEAD**-0.5 * math.log2(math.e)
LOWEST = -1e30
MESH = pl.DeviceIdType.MESH

SEM_PROMPT, SEM_TREE, SEM_QUERY, SEM_OUT, SEM_PEERS, SEM_REST_PEERS = 0, 4, 8, 12, 16, 22
SEM_RELAYS, SEM_REST_RELAYS, SEMS = 28, 46, 64


def shift_of(slot):
    return slot + slot // 2 - 2 * (slot // 3)


def kernel(queries, branch, prompt, parents_in, counts_in, out, q_buf, kv, tree, top, total, acc, stage, prompt_in, parents, counts,
           send_sem, recv_sem, local_sem):
    leaf = lax.axis_index("leaf")
    x = lax.rem(leaf, LINE)
    line = leaf - x
    y = lax.rem(leaf // LINE, LINE)
    z = leaf // (LINE * LINE)

    peers = [(z * LINE + lax.rem(y + d, LINE)) * LINE + x for d in (1, 3, 2)]
    peers += [(lax.rem(z + d, LINE) * LINE + y) * LINE + x for d in (1, 3, 2)]
    line_devices = [line + lax.rem(x + d, LINE) for d in range(1, LINE)]

    barrier = pltpu.get_barrier_semaphore()
    partners = line_devices + peers
    for device in partners:
        pl.semaphore_signal(barrier, inc=1, device_id={"leaf": device}, device_id_type=MESH)

    def columns(place, width):
        return pl.ds(pl.multiple_of(place * width, width), width)

    whole_prompt = pltpu.make_async_copy(prompt, prompt_in, local_sem.at[4])
    own_prompt = pltpu.make_async_copy(prompt.at[:, :, columns(x, HEAD)], kv.at[:, pl.ds(0, BLOCK), :], local_sem.at[0])
    small = [pltpu.make_async_copy(parents_in, parents, local_sem.at[5]), pltpu.make_async_copy(counts_in, counts, local_sem.at[6])]
    own_query = pltpu.make_async_copy(queries.at[:, columns(x, WIDTH)], q_buf.at[0], local_sem.at[1])
    own_tree = pltpu.make_async_copy(branch.at[:, :, columns(x, HEAD)], tree.at[:, pl.ds(0, BLOCK), :], local_sem.at[2])
    own_out = pltpu.make_async_copy(stage.at[0], out.at[:, columns(x, WIDTH)], local_sem.at[3])
    own_prompt.start()
    own_query.start()
    own_tree.start()
    whole_prompt.start()
    for copy in small:
        copy.start()
    own_prompt.wait()
    whole_prompt.wait()
    pl.semaphore_wait(barrier, len(partners))

    def to_line(slot, source, target, first):
        there = lax.rem(x + shift_of(slot), LINE)
        return pltpu.make_async_remote_copy(
            src_ref=source(there), dst_ref=target, send_sem=send_sem.at[first + slot], recv_sem=recv_sem.at[first + slot],
            device_id={"leaf": line + there}, device_id_type=MESH)

    def prompt_copy(slot):
        return to_line(slot, lambda there: prompt_in.at[:, :, columns(there, HEAD)], kv.at[:, pl.ds(AT_REST + (slot - 1) * BLOCK, BLOCK), :], SEM_PROMPT)

    def tree_copy(slot):
        return to_line(slot, lambda there: branch.at[:, :, columns(there, HEAD)], tree.at[:, pl.ds(slot * BLOCK, BLOCK), :], SEM_TREE)

    def query_copy(slot):
        return to_line(slot, lambda there: queries.at[:, columns(there, WIDTH)], q_buf.at[slot], SEM_QUERY)

    def out_copy(slot):
        there = lax.rem(x - shift_of(slot) + LINE, LINE)
        return pltpu.make_async_remote_copy(
            src_ref=stage.at[slot], dst_ref=out.at[:, columns(x, WIDTH)], send_sem=send_sem.at[SEM_OUT + slot],
            recv_sem=recv_sem.at[SEM_OUT + slot], device_id={"leaf": line + there}, device_id_type=MESH)

    def peer_copy(rest, peer):
        start, length = (AT_REST, REST) if rest else (0, BLOCK)
        to = (AT_REST_PEERS if rest else AT_PEERS) + peer * length
        sem = (SEM_REST_PEERS if rest else SEM_PEERS) + peer
        return pltpu.make_async_remote_copy(
            src_ref=kv.at[:, pl.ds(start, length), :], dst_ref=kv.at[:, pl.ds(to, length), :], send_sem=send_sem.at[sem],
            recv_sem=recv_sem.at[sem], device_id={"leaf": peers[peer]}, device_id_type=MESH)

    def relay_copy(rest, peer, turn):
        half = (REST if rest else BLOCK) // 2
        start = (AT_REST_PEERS if rest else AT_PEERS) + (2 * peer + peer // 3) * half
        index = 3 * peer + turn
        sem = (SEM_REST_RELAYS if rest else SEM_RELAYS) + index
        to = (AT_REST_RELAYS if rest else AT_RELAYS) + index * half
        return pltpu.make_async_remote_copy(
            src_ref=kv.at[:, pl.ds(start, half), :], dst_ref=kv.at[:, pl.ds(to, half), :], send_sem=send_sem.at[sem],
            recv_sem=recv_sem.at[sem], device_id={"leaf": peers[3 - peer // 3 * 3 + turn]}, device_id_type=MESH)

    NEAR, FAR = (0, 3, 1, 4), (2, 5)

    def relay(rest, which):
        for peer in which:
            peer_copy(rest, peer).wait_recv()
            for turn in range(3):
                relay_copy(rest, peer, turn).start()

    for slot in (1, 2):
        prompt_copy(slot).start()
    for peer in NEAR + FAR:
        peer_copy(0, peer).start()
    prompt_copy(3).start()
    for slot in (1, 2):
        query_copy(slot).start()
    for copy in small:
        copy.wait()

    parent = [parents[line + i] - line for i in range(LINE)]
    above = {}
    for b in range(1, LINE):
        for c in range(b):
            seen = jnp.where(parent[b] == c, 1, 0)
            for mid in range(c + 1, b):
                seen = jnp.maximum(seen, jnp.where(parent[b] == mid, above[mid, c], 0))
            above[b, c] = seen

    def masked(scores, slot):
        mine = lax.rem(x - shift_of(slot) + LINE, LINE)
        row = lax.broadcasted_iota(jnp.int32, (BLOCK, BLOCK), 0)
        column = lax.broadcasted_iota(jnp.int32, (BLOCK, BLOCK), 1)
        heads = [[] for _ in range(GROUP)]
        for other in range(LINE):
            block = lax.rem(x - shift_of(other) + LINE, LINE)
            linked = jnp.int32(0)
            for (b, c), seen in above.items():
                linked = jnp.where((mine == b) & (block == c), seen, linked)
            limit = linked * counts[line + block]
            limits = jnp.where(mine == block, row + 1, limit)
            for g in range(GROUP):
                piece = scores[g * BLOCK:(g + 1) * BLOCK, other * BLOCK:(other + 1) * BLOCK]
                heads[g].append(jnp.where(column < limits, piece, LOWEST))
        return jnp.concatenate([jnp.concatenate(head, axis=1) for head in heads], axis=0)

    def score(q, keys):
        return lax.dot_general(q, keys, (((1,), (1,)), ((), ())), preferred_element_type=jnp.float32)

    def attend(slot, chunks, first=False, last=False):
        q = jnp.concatenate([q_buf[slot, :, g * HEAD:(g + 1) * HEAD] for g in range(GROUP)], axis=0)
        if first:
            m, l, a = jnp.full((ROWS, HEAD), LOWEST, jnp.float32), jnp.zeros((ROWS, HEAD), jnp.float32), jnp.zeros((ROWS, HEAD), jnp.float32)
        else:
            m, l, a = top[slot], total[slot], acc[slot]

        def scores_of(chunk):
            buffer, start, length = chunk
            s = score(q, buffer[0, pl.ds(start, length), :])
            return masked(s, slot) if buffer is tree else s

        s = scores_of(chunks[0])
        for n, (buffer, start, length) in enumerate(chunks):
            following = scores_of(chunks[n + 1]) if n + 1 < len(chunks) else None
            new = jnp.maximum(m, jnp.broadcast_to(jnp.max(s, axis=1, keepdims=True), (ROWS, HEAD)))
            factor = jnp.exp2((m - new) * TO_EXP2)
            weights = jnp.concatenate(
                [jnp.exp2((s[:, i:i + HEAD] - new) * TO_EXP2).astype(jnp.bfloat16) for i in range(0, length, HEAD)], axis=1)
            values = buffer[1, pl.ds(start, length), :]
            both = jnp.dot(weights, jnp.concatenate([values, jnp.ones_like(values)], axis=1), preferred_element_type=jnp.float32)
            a = a * factor + both[:, :HEAD]
            l = l * factor + both[:, HEAD:]
            m, s = new, following
        if not last:
            top[slot], total[slot], acc[slot] = m, l, a
            return
        mine = lax.rem(x - shift_of(slot) + LINE, LINE)
        live = lax.broadcasted_iota(jnp.int32, (BLOCK, HEAD), 0) < counts[line + mine]
        for g in range(GROUP):
            rows = slice(g * BLOCK, (g + 1) * BLOCK)
            stage[slot, :, g * HEAD:(g + 1) * HEAD] = jnp.where(live, a[rows] / l[rows], 0.0).astype(stage.dtype)

    def chunks(*lengths):
        start, found = lengths[0], []
        for length in lengths[1:]:
            found.append((kv, start, length))
            start += length
        return found

    first = chunks(0, 768)
    second = chunks(768, 768, 768) + [(tree, 0, LINE * BLOCK)]
    third = chunks(2304, 768, 768, 768)
    fourth = chunks(4608, 1024, 1024, 1024, 512)

    relay(0, NEAR)
    relay(0, FAR)
    query_copy(3).start()
    for slot in (1, 2, 3):
        tree_copy(slot).start()
    own_query.wait()
    attend(0, first, first=True)
    for slot in (1, 2, 3):
        prompt_copy(slot).wait_recv()
    for peer in NEAR + FAR:
        peer_copy(1, peer).start()
    for slot in (1, 2):
        query_copy(slot).wait_recv()

    def near_first(i, c):
        attend(i + 1, first, first=True)
        return c

    lax.fori_loop(0, 2, near_first, 0)
    for peer in range(PEERS):
        for turn in range(3):
            relay_copy(0, peer, turn).wait_recv()
    own_tree.wait()
    for slot in (1, 2, 3):
        tree_copy(slot).wait_recv()

    def near_second(i, c):
        attend(i, second)

        @pl.when(i == 1)
        def _():
            relay(1, NEAR)

        return c

    lax.fori_loop(0, 3, near_second, 0)
    query_copy(3).wait_recv()
    attend(3, first + second, first=True)
    relay(1, FAR)

    def all_third(i, c):
        attend(i, third)
        return c

    lax.fori_loop(0, LINE, all_third, 0)
    for peer in range(PEERS):
        for turn in range(3):
            relay_copy(1, peer, turn).wait_recv()

    def final(i, c):
        slot = 3 - i
        attend(slot, fourth, last=True)

        @pl.when(i < 3)
        def _():
            out_copy(slot).start()

        return c

    lax.fori_loop(0, 4, final, 0)
    own_out.start()
    for slot in (1, 2, 3):
        prompt_copy(slot).wait_send()
        tree_copy(slot).wait_send()
        query_copy(slot).wait_send()
        out_copy(slot).wait_send()
    for rest in range(2):
        for peer in range(PEERS):
            peer_copy(rest, peer).wait_send()
            for turn in range(3):
                relay_copy(rest, peer, turn).wait_send()
    for slot in (1, 2, 3):
        out_copy(slot).wait_recv()
    own_out.wait()


def shards(queries, branch, prompt, parents, counts):
    return pl.pallas_call(
        kernel,
        out_shape=jax.ShapeDtypeStruct(queries.shape, queries.dtype),
        in_specs=[pl.BlockSpec(memory_space=pltpu.HBM)] * 5,
        out_specs=pl.BlockSpec(memory_space=pltpu.HBM),
        scratch_shapes=[
            pltpu.VMEM((LINE, BLOCK, WIDTH), jnp.bfloat16),
            pltpu.VMEM((2, PROMPT, HEAD), jnp.bfloat16),
            pltpu.VMEM((2, LINE * BLOCK, HEAD), jnp.bfloat16),
            pltpu.VMEM((LINE, ROWS, HEAD), jnp.float32),
            pltpu.VMEM((LINE, ROWS, HEAD), jnp.float32),
            pltpu.VMEM((LINE, ROWS, HEAD), jnp.float32),
            pltpu.VMEM((LINE, BLOCK, WIDTH), jnp.bfloat16),
            pltpu.VMEM((2, BLOCK, KV_HEADS * HEAD), jnp.bfloat16),
            pltpu.SMEM((64,), jnp.int32),
            pltpu.SMEM((64,), jnp.int32),
            pltpu.SemaphoreType.DMA((SEMS,)),
            pltpu.SemaphoreType.DMA((SEMS,)),
            pltpu.SemaphoreType.DMA((7,)),
        ],
        compiler_params=pltpu.CompilerParams(
            collective_id=0, has_side_effects=True, vmem_limit_bytes=52 * 2**20
        ),
    )(queries, branch, prompt, parents, counts)


def solution(mesh):
    placed = (
        P(("rep", "leaf"), None),
        P(None, ("rep", "leaf"), None),
        P(None, ("rep", "leaf"), None),
        P("rep"),
        P("rep"),
    )
    return jax.shard_map(
        shards, mesh=mesh, in_specs=placed, out_specs=P(("rep", "leaf"), None), check_vma=False
    )
```

```python
import functools
import math

import jax
import jax.numpy as jnp
from jax import lax
from jax.experimental import pallas as pl
from jax.experimental.pallas import tpu as pltpu
from jax.sharding import PartitionSpec as P

QUERY_HEADS = 28
KV_HEADS = 4
HEAD = 128
BLOCK = 128
LINE = 4
GROUP = QUERY_HEADS // KV_HEADS
WIDTH = GROUP * HEAD
ROWS = GROUP * BLOCK
PLANE = 16
PEERS = 6
RELAYS = 18
PROMPT = PLANE * LINE * BLOCK
REST = (LINE - 1) * BLOCK
AT_PEERS = BLOCK
AT_REST = AT_PEERS + PEERS * BLOCK
AT_RELAYS = AT_REST + REST
AT_REST_PEERS = AT_RELAYS + RELAYS * BLOCK // 2
AT_REST_RELAYS = AT_REST_PEERS + PEERS * REST
TO_EXP2 = HEAD**-0.5 * math.log2(math.e)
LOWEST = -1e30
MESH = pl.DeviceIdType.MESH

SEM_PROMPT, SEM_TREE, SEM_QUERY, SEM_OUT, SEM_PEERS, SEM_REST_PEERS = 0, 4, 8, 12, 16, 22
SEM_RELAYS, SEM_REST_RELAYS, SEMS = 28, 46, 64


def shift_of(slot):
    return slot + slot // 2 - 2 * (slot // 3)


def kernel(queries, branch, prompt, parents_in, counts_in, out, q_buf, kv, tree, top, total, acc, stage, prompt_in, parents, counts,
           send_sem, recv_sem, local_sem):
    leaf = lax.axis_index("leaf")
    x = lax.rem(leaf, LINE)
    line = leaf - x
    y = lax.rem(leaf // LINE, LINE)
    z = leaf // (LINE * LINE)

    peers = [(z * LINE + lax.rem(y + d, LINE)) * LINE + x for d in (1, 3, 2)]
    peers += [(lax.rem(z + d, LINE) * LINE + y) * LINE + x for d in (1, 3, 2)]
    line_devices = [line + lax.rem(x + d, LINE) for d in range(1, LINE)]

    barrier = pltpu.get_barrier_semaphore()
    partners = line_devices + peers
    for device in partners:
        pl.semaphore_signal(barrier, inc=1, device_id={"leaf": device}, device_id_type=MESH)

    def columns(place, width):
        return pl.ds(pl.multiple_of(place * width, width), width)

    whole_prompt = pltpu.make_async_copy(prompt, prompt_in, local_sem.at[4])
    own_prompt = pltpu.make_async_copy(prompt.at[:, :, columns(x, HEAD)], kv.at[:, pl.ds(0, BLOCK), :], local_sem.at[0])
    small = [pltpu.make_async_copy(parents_in, parents, local_sem.at[5]), pltpu.make_async_copy(counts_in, counts, local_sem.at[6])]
    own_query = pltpu.make_async_copy(queries.at[:, columns(x, WIDTH)], q_buf.at[0], local_sem.at[1])
    own_tree = pltpu.make_async_copy(branch.at[:, :, columns(x, HEAD)], tree.at[:, pl.ds(0, BLOCK), :], local_sem.at[2])
    own_out = pltpu.make_async_copy(stage.at[0], out.at[:, columns(x, WIDTH)], local_sem.at[3])
    own_prompt.start()
    own_query.start()
    own_tree.start()
    whole_prompt.start()
    for copy in small:
        copy.start()
    own_prompt.wait()
    whole_prompt.wait()
    pl.semaphore_wait(barrier, len(partners))

    def to_line(slot, source, target, first):
        there = lax.rem(x + shift_of(slot), LINE)
        return pltpu.make_async_remote_copy(
            src_ref=source(there), dst_ref=target, send_sem=send_sem.at[first + slot], recv_sem=recv_sem.at[first + slot],
            device_id={"leaf": line + there}, device_id_type=MESH)

    def prompt_copy(slot):
        return to_line(slot, lambda there: prompt_in.at[:, :, columns(there, HEAD)], kv.at[:, pl.ds(AT_REST + (slot - 1) * BLOCK, BLOCK), :], SEM_PROMPT)

    def tree_copy(slot):
        return to_line(slot, lambda there: branch.at[:, :, columns(there, HEAD)], tree.at[:, pl.ds(slot * BLOCK, BLOCK), :], SEM_TREE)

    def query_copy(slot):
        return to_line(slot, lambda there: queries.at[:, columns(there, WIDTH)], q_buf.at[slot], SEM_QUERY)

    def out_copy(slot):
        there = lax.rem(x - shift_of(slot) + LINE, LINE)
        return pltpu.make_async_remote_copy(
            src_ref=stage.at[slot], dst_ref=out.at[:, columns(x, WIDTH)], send_sem=send_sem.at[SEM_OUT + slot],
            recv_sem=recv_sem.at[SEM_OUT + slot], device_id={"leaf": line + there}, device_id_type=MESH)

    def peer_copy(rest, peer):
        start, length = (AT_REST, REST) if rest else (0, BLOCK)
        to = (AT_REST_PEERS if rest else AT_PEERS) + peer * length
        sem = (SEM_REST_PEERS if rest else SEM_PEERS) + peer
        return pltpu.make_async_remote_copy(
            src_ref=kv.at[:, pl.ds(start, length), :], dst_ref=kv.at[:, pl.ds(to, length), :], send_sem=send_sem.at[sem],
            recv_sem=recv_sem.at[sem], device_id={"leaf": peers[peer]}, device_id_type=MESH)

    def relay_copy(rest, peer, turn):
        half = (REST if rest else BLOCK) // 2
        start = (AT_REST_PEERS if rest else AT_PEERS) + (2 * peer + peer // 3) * half
        index = 3 * peer + turn
        sem = (SEM_REST_RELAYS if rest else SEM_RELAYS) + index
        to = (AT_REST_RELAYS if rest else AT_RELAYS) + index * half
        return pltpu.make_async_remote_copy(
            src_ref=kv.at[:, pl.ds(start, half), :], dst_ref=kv.at[:, pl.ds(to, half), :], send_sem=send_sem.at[sem],
            recv_sem=recv_sem.at[sem], device_id={"leaf": peers[3 - peer // 3 * 3 + turn]}, device_id_type=MESH)

    NEAR, FAR = (0, 3, 1, 4), (2, 5)

    def relay(rest, which):
        for peer in which:
            peer_copy(rest, peer).wait_recv()
            for turn in range(3):
                relay_copy(rest, peer, turn).start()

    for slot in (1, 2):
        prompt_copy(slot).start()
    for peer in NEAR + FAR:
        peer_copy(0, peer).start()
    prompt_copy(3).start()
    for slot in (1, 2):
        query_copy(slot).start()
    for copy in small:
        copy.wait()

    parent = [parents[line + i] - line for i in range(LINE)]
    above = {}
    for b in range(1, LINE):
        for c in range(b):
            seen = jnp.where(parent[b] == c, 1, 0)
            for mid in range(c + 1, b):
                seen = jnp.maximum(seen, jnp.where(parent[b] == mid, above[mid, c], 0))
            above[b, c] = seen

    def masked(scores, slot):
        mine = lax.rem(x - shift_of(slot) + LINE, LINE)
        row = lax.broadcasted_iota(jnp.int32, (BLOCK, BLOCK), 0)
        column = lax.broadcasted_iota(jnp.int32, (BLOCK, BLOCK), 1)
        heads = [[] for _ in range(GROUP)]
        for other in range(LINE):
            block = lax.rem(x - shift_of(other) + LINE, LINE)
            linked = jnp.int32(0)
            for (b, c), seen in above.items():
                linked = jnp.where((mine == b) & (block == c), seen, linked)
            limit = linked * counts[line + block]
            limits = jnp.where(mine == block, row + 1, limit)
            for g in range(GROUP):
                piece = scores[g * BLOCK:(g + 1) * BLOCK, other * BLOCK:(other + 1) * BLOCK]
                heads[g].append(jnp.where(column < limits, piece, LOWEST))
        return jnp.concatenate([jnp.concatenate(head, axis=1) for head in heads], axis=0)

    def score(q, keys):
        return lax.dot_general(q, keys, (((1,), (1,)), ((), ())), preferred_element_type=jnp.float32)

    def begin(slot):
        return jnp.full((ROWS, HEAD), LOWEST, jnp.float32), jnp.zeros((ROWS, HEAD), jnp.float32), jnp.zeros((ROWS, HEAD), jnp.float32)

    def resume(slot):
        return top[slot], total[slot], acc[slot]

    def keep(slot, m, l, a):
        top[slot], total[slot], acc[slot] = m, l, a

    def finish(slot, m, l, a):
        mine = lax.rem(x - shift_of(slot) + LINE, LINE)
        live = lax.broadcasted_iota(jnp.int32, (BLOCK, HEAD), 0) < counts[line + mine]
        for g in range(GROUP):
            rows = slice(g * BLOCK, (g + 1) * BLOCK)
            stage[slot, :, g * HEAD:(g + 1) * HEAD] = jnp.where(live, a[rows] / l[rows], 0.0).astype(stage.dtype)

    def attend(slots, chunks, load=resume, store=keep):
        tasks = [(slot, n) for slot in slots for n in range(len(chunks))]

        def scores_of(slot, n):
            buffer, start, length = chunks[n]
            q = jnp.concatenate([q_buf[slot, :, g * HEAD:(g + 1) * HEAD] for g in range(GROUP)], axis=0)
            s = score(q, buffer[0, pl.ds(start, length), :])
            return masked(s, slot) if buffer is tree else s

        s = scores_of(*tasks[0])
        for task, (slot, n) in enumerate(tasks):
            following = scores_of(*tasks[task + 1]) if task + 1 < len(tasks) else None
            buffer, start, length = chunks[n]
            if n == 0:
                m, l, a = load(slot)
            new = jnp.maximum(m, jnp.broadcast_to(jnp.max(s, axis=1, keepdims=True), (ROWS, HEAD)))
            factor = jnp.exp2((m - new) * TO_EXP2)
            weights = jnp.concatenate(
                [jnp.exp2((s[:, i:i + HEAD] - new) * TO_EXP2).astype(jnp.bfloat16) for i in range(0, length, HEAD)], axis=1)
            values = buffer[1, pl.ds(start, length), :]
            both = jnp.dot(weights, jnp.concatenate([values, jnp.ones_like(values)], axis=1), preferred_element_type=jnp.float32)
            a = a * factor + both[:, :HEAD]
            l = l * factor + both[:, HEAD:]
            m, s = new, following
            if n == len(chunks) - 1:
                store(slot, m, l, a)

    def chunks(*lengths):
        start, found = lengths[0], []
        for length in lengths[1:]:
            found.append((kv, start, length))
            start += length
        return found

    relay(0, NEAR)
    relay(0, FAR)
    query_copy(3).start()
    own_query.wait()
    attend([0], chunks(0, 384, 384), load=begin)
    for slot in (1, 2, 3):
        prompt_copy(slot).wait_recv()
    for peer in NEAR + FAR:
        peer_copy(1, peer).start()
    attend([0], chunks(768, 512))
    for slot in (1, 2):
        query_copy(slot).wait_recv()
    for slot in (1, 2, 3):
        tree_copy(slot).start()
    attend([1, 2], chunks(0, 512, 768), load=begin)
    for peer in range(PEERS):
        for turn in range(3):
            relay_copy(0, peer, turn).wait_recv()
    attend([0, 1, 2], chunks(1280, 1024))
    relay(1, NEAR)
    query_copy(3).wait_recv()
    attend([3], chunks(0, 512, 768, 1024), load=begin)
    relay(1, FAR)
    own_tree.wait()
    for slot in (1, 2, 3):
        tree_copy(slot).wait_recv()

    def middle(i, c):
        attend([i], chunks(2304, 768, 768, 768) + [(tree, 0, LINE * BLOCK)])
        return c

    lax.fori_loop(0, LINE, middle, 0)
    for peer in range(PEERS):
        for turn in range(3):
            relay_copy(1, peer, turn).wait_recv()

    def final(i, c):
        slot = 3 - i
        attend([slot], chunks(4608, 1024, 1024, 1024, 512), store=finish)

        @pl.when(i < 3)
        def _():
            out_copy(slot).start()

        return c

    lax.fori_loop(0, 4, final, 0)
    own_out.start()
    for slot in (1, 2, 3):
        prompt_copy(slot).wait_send()
        tree_copy(slot).wait_send()
        query_copy(slot).wait_send()
        out_copy(slot).wait_send()
    for rest in range(2):
        for peer in range(PEERS):
            peer_copy(rest, peer).wait_send()
            for turn in range(3):
                relay_copy(rest, peer, turn).wait_send()
    for slot in (1, 2, 3):
        out_copy(slot).wait_recv()
    own_out.wait()


def shards(queries, branch, prompt, parents, counts):
    return pl.pallas_call(
        kernel,
        out_shape=jax.ShapeDtypeStruct(queries.shape, queries.dtype),
        in_specs=[pl.BlockSpec(memory_space=pltpu.HBM)] * 5,
        out_specs=pl.BlockSpec(memory_space=pltpu.HBM),
        scratch_shapes=[
            pltpu.VMEM((LINE, BLOCK, WIDTH), jnp.bfloat16),
            pltpu.VMEM((2, PROMPT, HEAD), jnp.bfloat16),
            pltpu.VMEM((2, LINE * BLOCK, HEAD), jnp.bfloat16),
            pltpu.VMEM((LINE, ROWS, HEAD), jnp.float32),
            pltpu.VMEM((LINE, ROWS, HEAD), jnp.float32),
            pltpu.VMEM((LINE, ROWS, HEAD), jnp.float32),
            pltpu.VMEM((LINE, BLOCK, WIDTH), jnp.bfloat16),
            pltpu.VMEM((2, BLOCK, KV_HEADS * HEAD), jnp.bfloat16),
            pltpu.SMEM((64,), jnp.int32),
            pltpu.SMEM((64,), jnp.int32),
            pltpu.SemaphoreType.DMA((SEMS,)),
            pltpu.SemaphoreType.DMA((SEMS,)),
            pltpu.SemaphoreType.DMA((7,)),
        ],
        compiler_params=pltpu.CompilerParams(
            collective_id=0, has_side_effects=True, vmem_limit_bytes=60 * 2**20
        ),
    )(queries, branch, prompt, parents, counts)


def solution(mesh):
    placed = (
        P(("rep", "leaf"), None),
        P(None, ("rep", "leaf"), None),
        P(None, ("rep", "leaf"), None),
        P("rep"),
        P("rep"),
    )
    return jax.shard_map(
        shards, mesh=mesh, in_specs=placed, out_specs=P(("rep", "leaf"), None), check_vma=False
    )
```

```python
import functools
import math

import jax
import jax.numpy as jnp
from jax import lax
from jax.experimental import pallas as pl
from jax.experimental.pallas import tpu as pltpu
from jax.sharding import PartitionSpec as P

QUERY_HEADS = 28
KV_HEADS = 4
HEAD = 128
BLOCK = 128
LINE = 4
GROUP = QUERY_HEADS // KV_HEADS
WIDTH = GROUP * HEAD
ROWS = GROUP * BLOCK
PLANE = 16
PEERS = 6
RELAYS = 18
PROMPT = PLANE * LINE * BLOCK
REST = (LINE - 1) * BLOCK
AT_PEERS = BLOCK
AT_REST = AT_PEERS + PEERS * BLOCK
AT_RELAYS = AT_REST + REST
AT_REST_PEERS = AT_RELAYS + RELAYS * BLOCK // 2
AT_REST_RELAYS = AT_REST_PEERS + PEERS * REST
TO_EXP2 = HEAD**-0.5 * math.log2(math.e)
LOWEST = -1e30
MESH = pl.DeviceIdType.MESH

SEM_PROMPT, SEM_TREE, SEM_QUERY, SEM_OUT, SEM_PEERS, SEM_REST_PEERS = 0, 4, 8, 12, 16, 22
SEM_RELAYS, SEM_REST_RELAYS, SEMS = 28, 46, 64


def shift_of(slot):
    return slot + slot // 2 - 2 * (slot // 3)


def kernel(queries, branch, prompt, parents_in, counts_in, out, q_buf, kv, tree, top, total, acc, stage, prompt_in, parents, counts,
           send_sem, recv_sem, local_sem):
    leaf = lax.axis_index("leaf")
    x = lax.rem(leaf, LINE)
    line = leaf - x
    y = lax.rem(leaf // LINE, LINE)
    z = leaf // (LINE * LINE)

    peers = [(z * LINE + lax.rem(y + d, LINE)) * LINE + x for d in (1, 3, 2)]
    peers += [(lax.rem(z + d, LINE) * LINE + y) * LINE + x for d in (1, 3, 2)]
    line_devices = [line + lax.rem(x + d, LINE) for d in range(1, LINE)]

    barrier = pltpu.get_barrier_semaphore()
    partners = line_devices + peers
    for device in partners:
        pl.semaphore_signal(barrier, inc=1, device_id={"leaf": device}, device_id_type=MESH)

    def columns(place, width):
        return pl.ds(pl.multiple_of(place * width, width), width)

    whole_prompt = pltpu.make_async_copy(prompt, prompt_in, local_sem.at[4])
    own_prompt = pltpu.make_async_copy(prompt.at[:, :, columns(x, HEAD)], kv.at[:, pl.ds(0, BLOCK), :], local_sem.at[0])
    small = [pltpu.make_async_copy(parents_in, parents, local_sem.at[5]), pltpu.make_async_copy(counts_in, counts, local_sem.at[6])]
    own_query = pltpu.make_async_copy(queries.at[:, columns(x, WIDTH)], q_buf.at[0], local_sem.at[1])
    own_tree = pltpu.make_async_copy(branch.at[:, :, columns(x, HEAD)], tree.at[:, pl.ds(0, BLOCK), :], local_sem.at[2])
    own_out = pltpu.make_async_copy(stage.at[0], out.at[:, columns(x, WIDTH)], local_sem.at[3])
    own_prompt.start()
    own_query.start()
    own_tree.start()
    whole_prompt.start()
    for copy in small:
        copy.start()
    own_prompt.wait()
    whole_prompt.wait()
    pl.semaphore_wait(barrier, len(partners))

    def to_line(slot, source, target, first):
        there = lax.rem(x + shift_of(slot), LINE)
        return pltpu.make_async_remote_copy(
            src_ref=source(there), dst_ref=target, send_sem=send_sem.at[first + slot], recv_sem=recv_sem.at[first + slot],
            device_id={"leaf": line + there}, device_id_type=MESH)

    def prompt_copy(slot):
        return to_line(slot, lambda there: prompt_in.at[:, :, columns(there, HEAD)], kv.at[:, pl.ds(AT_REST + (slot - 1) * BLOCK, BLOCK), :], SEM_PROMPT)

    def tree_copy(slot):
        return to_line(slot, lambda there: branch.at[:, :, columns(there, HEAD)], tree.at[:, pl.ds(slot * BLOCK, BLOCK), :], SEM_TREE)

    def query_copy(slot):
        return to_line(slot, lambda there: queries.at[:, columns(there, WIDTH)], q_buf.at[slot], SEM_QUERY)

    def out_copy(slot):
        there = lax.rem(x - shift_of(slot) + LINE, LINE)
        return pltpu.make_async_remote_copy(
            src_ref=stage.at[slot], dst_ref=out.at[:, columns(x, WIDTH)], send_sem=send_sem.at[SEM_OUT + slot],
            recv_sem=recv_sem.at[SEM_OUT + slot], device_id={"leaf": line + there}, device_id_type=MESH)

    def peer_copy(rest, peer):
        start, length = (AT_REST, REST) if rest else (0, BLOCK)
        to = (AT_REST_PEERS if rest else AT_PEERS) + peer * length
        sem = (SEM_REST_PEERS if rest else SEM_PEERS) + peer
        return pltpu.make_async_remote_copy(
            src_ref=kv.at[:, pl.ds(start, length), :], dst_ref=kv.at[:, pl.ds(to, length), :], send_sem=send_sem.at[sem],
            recv_sem=recv_sem.at[sem], device_id={"leaf": peers[peer]}, device_id_type=MESH)

    def relay_copy(rest, peer, turn):
        half = (REST if rest else BLOCK) // 2
        start = (AT_REST_PEERS if rest else AT_PEERS) + (2 * peer + peer // 3) * half
        index = 3 * (0, 2, 4, 1, 3, 5)[peer] + turn
        sem = (SEM_REST_RELAYS if rest else SEM_RELAYS) + index
        to = (AT_REST_RELAYS if rest else AT_RELAYS) + index * half
        return pltpu.make_async_remote_copy(
            src_ref=kv.at[:, pl.ds(start, half), :], dst_ref=kv.at[:, pl.ds(to, half), :], send_sem=send_sem.at[sem],
            recv_sem=recv_sem.at[sem], device_id={"leaf": peers[3 - peer // 3 * 3 + turn]}, device_id_type=MESH)

    NEAR, FAR = (0, 3, 1, 4), (2, 5)

    def relay(rest, which):
        for peer in which:
            peer_copy(rest, peer).wait_recv()
            for turn in range(3):
                relay_copy(rest, peer, turn).start()

    for slot in (1, 2):
        prompt_copy(slot).start()
    for peer in NEAR + FAR:
        peer_copy(0, peer).start()
    prompt_copy(3).start()
    for slot in (1, 2):
        query_copy(slot).start()
    for copy in small:
        copy.wait()

    parent = [parents[line + i] - line for i in range(LINE)]
    above = {}
    for b in range(1, LINE):
        for c in range(b):
            seen = jnp.where(parent[b] == c, 1, 0)
            for mid in range(c + 1, b):
                seen = jnp.maximum(seen, jnp.where(parent[b] == mid, above[mid, c], 0))
            above[b, c] = seen

    def masked(scores, slot):
        mine = lax.rem(x - shift_of(slot) + LINE, LINE)
        row = lax.broadcasted_iota(jnp.int32, (BLOCK, BLOCK), 0)
        column = lax.broadcasted_iota(jnp.int32, (BLOCK, BLOCK), 1)
        heads = [[] for _ in range(GROUP)]
        for other in range(LINE):
            block = lax.rem(x - shift_of(other) + LINE, LINE)
            linked = jnp.int32(0)
            for (b, c), seen in above.items():
                linked = jnp.where((mine == b) & (block == c), seen, linked)
            limit = linked * counts[line + block]
            limits = jnp.where(mine == block, row + 1, limit)
            for g in range(GROUP):
                piece = scores[g * BLOCK:(g + 1) * BLOCK, other * BLOCK:(other + 1) * BLOCK]
                heads[g].append(jnp.where(column < limits, piece, LOWEST))
        return jnp.concatenate([jnp.concatenate(head, axis=1) for head in heads], axis=0)

    def score(q, keys):
        return lax.dot_general(q, keys, (((1,), (1,)), ((), ())), preferred_element_type=jnp.float32)

    def begin(slot):
        return jnp.full((ROWS, HEAD), LOWEST, jnp.float32), jnp.zeros((ROWS, HEAD), jnp.float32), jnp.zeros((ROWS, HEAD), jnp.float32)

    def resume(slot):
        return top[slot], total[slot], acc[slot]

    def keep(slot, m, l, a):
        top[slot], total[slot], acc[slot] = m, l, a

    def finish(slot, m, l, a):
        mine = lax.rem(x - shift_of(slot) + LINE, LINE)
        live = lax.broadcasted_iota(jnp.int32, (BLOCK, HEAD), 0) < counts[line + mine]
        for g in range(GROUP):
            rows = slice(g * BLOCK, (g + 1) * BLOCK)
            stage[slot, :, g * HEAD:(g + 1) * HEAD] = jnp.where(live, a[rows] / l[rows], 0.0).astype(stage.dtype)

    def attend(slots, chunks, load=resume, store=keep):
        tasks = [(slot, n) for slot in slots for n in range(len(chunks))]

        def scores_of(slot, n):
            buffer, start, length = chunks[n]
            q = jnp.concatenate([q_buf[slot, :, g * HEAD:(g + 1) * HEAD] for g in range(GROUP)], axis=0)
            s = score(q, buffer[0, pl.ds(start, length), :])
            return masked(s, slot) if buffer is tree else s

        s = scores_of(*tasks[0])
        for task, (slot, n) in enumerate(tasks):
            following = scores_of(*tasks[task + 1]) if task + 1 < len(tasks) else None
            buffer, start, length = chunks[n]
            if n == 0:
                m, l, a = load(slot)
            new = jnp.maximum(m, jnp.broadcast_to(jnp.max(s, axis=1, keepdims=True), (ROWS, HEAD)))
            factor = jnp.exp2((m - new) * TO_EXP2)
            weights = jnp.concatenate(
                [jnp.exp2((s[:, i:i + HEAD] - new) * TO_EXP2).astype(jnp.bfloat16) for i in range(0, length, HEAD)], axis=1)
            values = buffer[1, pl.ds(start, length), :]
            both = jnp.dot(weights, jnp.concatenate([values, jnp.ones_like(values)], axis=1), preferred_element_type=jnp.float32)
            a = a * factor + both[:, :HEAD]
            l = l * factor + both[:, HEAD:]
            m, s = new, following
            if n == len(chunks) - 1:
                store(slot, m, l, a)

    def chunks(*lengths):
        start, found = lengths[0], []
        for length in lengths[1:]:
            found.append((kv, start, length))
            start += length
        return found

    relay(0, NEAR)
    relay(0, FAR)
    query_copy(3).start()
    own_query.wait()
    attend([0], chunks(0, 384, 384), load=begin)
    for slot in (1, 2, 3):
        prompt_copy(slot).wait_recv()
    for peer in NEAR + FAR:
        peer_copy(1, peer).start()
    attend([0], chunks(768, 512))
    for slot in (1, 2):
        query_copy(slot).wait_recv()
    for slot in (1, 2, 3):
        tree_copy(slot).start()
    attend([1, 2], chunks(0, 512, 768), load=begin)
    for peer in range(PEERS):
        for turn in range(3):
            relay_copy(0, peer, turn).wait_recv()
    attend([0, 1, 2], chunks(1280, 1024))
    relay(1, NEAR)
    query_copy(3).wait_recv()
    attend([3], chunks(0, 512, 768, 1024), load=begin)
    relay(1, FAR)
    own_tree.wait()
    for slot in (1, 2, 3):
        tree_copy(slot).wait_recv()

    def middle(i, c):
        attend([i], chunks(2304, 768, 768, 768) + [(tree, 0, LINE * BLOCK)])
        return c

    lax.fori_loop(0, LINE, middle, 0)
    for peer in NEAR:
        for turn in range(3):
            relay_copy(1, peer, turn).wait_recv()
    attend([3, 2, 1], chunks(4608, 1024))
    for peer in FAR:
        for turn in range(3):
            relay_copy(1, peer, turn).wait_recv()

    def last(i, c):
        slot = 3 - i
        attend([slot], chunks(5632, 1024, 1024, 512), store=finish)
        out_copy(slot).start()
        return c

    lax.fori_loop(0, LINE - 1, last, 0)
    attend([0], chunks(4608, 1024, 1024, 1024, 512), store=finish)
    own_out.start()
    for slot in (1, 2, 3):
        prompt_copy(slot).wait_send()
        tree_copy(slot).wait_send()
        query_copy(slot).wait_send()
        out_copy(slot).wait_send()
    for rest in range(2):
        for peer in range(PEERS):
            peer_copy(rest, peer).wait_send()
            for turn in range(3):
                relay_copy(rest, peer, turn).wait_send()
    for slot in (1, 2, 3):
        out_copy(slot).wait_recv()
    own_out.wait()


def shards(queries, branch, prompt, parents, counts):
    return pl.pallas_call(
        kernel,
        out_shape=jax.ShapeDtypeStruct(queries.shape, queries.dtype),
        in_specs=[pl.BlockSpec(memory_space=pltpu.HBM)] * 5,
        out_specs=pl.BlockSpec(memory_space=pltpu.HBM),
        scratch_shapes=[
            pltpu.VMEM((LINE, BLOCK, WIDTH), jnp.bfloat16),
            pltpu.VMEM((2, PROMPT, HEAD), jnp.bfloat16),
            pltpu.VMEM((2, LINE * BLOCK, HEAD), jnp.bfloat16),
            pltpu.VMEM((LINE, ROWS, HEAD), jnp.float32),
            pltpu.VMEM((LINE, ROWS, HEAD), jnp.float32),
            pltpu.VMEM((LINE, ROWS, HEAD), jnp.float32),
            pltpu.VMEM((LINE, BLOCK, WIDTH), jnp.bfloat16),
            pltpu.VMEM((2, BLOCK, KV_HEADS * HEAD), jnp.bfloat16),
            pltpu.SMEM((64,), jnp.int32),
            pltpu.SMEM((64,), jnp.int32),
            pltpu.SemaphoreType.DMA((SEMS,)),
            pltpu.SemaphoreType.DMA((SEMS,)),
            pltpu.SemaphoreType.DMA((7,)),
        ],
        compiler_params=pltpu.CompilerParams(
            collective_id=0, has_side_effects=True, vmem_limit_bytes=60 * 2**20
        ),
    )(queries, branch, prompt, parents, counts)


def solution(mesh):
    placed = (
        P(("rep", "leaf"), None),
        P(None, ("rep", "leaf"), None),
        P(None, ("rep", "leaf"), None),
        P("rep"),
        P("rep"),
    )
    return jax.shard_map(
        shards, mesh=mesh, in_specs=placed, out_specs=P(("rep", "leaf"), None), check_vma=False
    )
```
